128 devices in a mesh: seq: 32 (over x, y, core), head: 4 (over z).
Axes of the slice: x: 4, y: 4, z: 4, core: 2. Of those that a mesh axis runs over, the one named last changes fastest.
Arguments:
- queries: bfloat16 [32768, 2048], P('seq', 'head'), may hold values from -6 to 6
- keys: bfloat16 [32768, 2048], P('seq', 'head'), may hold values from -6 to 6
- values: bfloat16 [32768, 2048], P('seq', 'head'), may hold values from -6 to 6
- out_weight: bfloat16 [4096, 2048], P('seq', 'head'), may hold values from -0.125 to 0.125
- out_grad: bfloat16 [32768, 4096], P('seq'), may hold values from -6 to 6
Outputs:
- mixed: bfloat16 [32768, 4096], P('seq', 'head')
- grad_queries: bfloat16 [32768, 2048], P('seq', 'head')
- grad_keys: bfloat16 [32768, 2048], P('seq', 'head')
- grad_values: bfloat16 [32768, 2048], P('seq', 'head')
- grad_weight: float32 [4096, 2048], P('seq', 'head')
The draws below stay inside these ranges and needn't reach their ends.
All inputs are finite; a program needn't handle non-finite values.
Results may differ from the reference program's by a relative error of at most 0.022.
Values may be sent and summed in bfloat16 or wider, within the bound.
A program may use at most 128 MiB of HBM per device.

```python
import jax
import jax.numpy as jnp
from jax import lax

D = 4096
HEAD_DIM = 128
BLOCK = 512
TOKENS = 32768
ATT_WIDTH = 2048
HEAD_GROUPS = 4


def with_spikes(result, stream_key, source, target, blocks, factor):
    owner, partner = [(jnp.arange(result.shape[dim]) // (result.shape[dim] // blocks)).reshape([-1 if axis == dim else 1 for axis in range(result.ndim)]) for dim in (source, target)]
    chosen = jax.random.permutation(stream_key, blocks)[partner]
    strong = (owner == chosen) | (owner == (partner + blocks // 2) % blocks)
    return jnp.where(strong, factor * result, result)


def level_of(key, shape, cuts, low, high):
    loudness = 1.0
    for dim, blocks in cuts:
        heights = jax.random.uniform(jax.random.fold_in(jax.random.fold_in(key, 6), dim), (blocks,), jnp.float32, low / len(cuts), high / len(cuts))
        loudness = loudness * jnp.repeat(jnp.exp(heights), shape[dim] // blocks).reshape((-1,) + (1,) * (len(shape) - 1 - dim))
    return loudness


def noise(rng, extent, deviation, most, shards=(), held_as=jnp.bfloat16):
    values = deviation * jax.random.normal(rng, extent, jnp.float32)
    if shards:
        values = values * level_of(rng, extent, shards, -0.22, 0.18)
    return jnp.clip(values, -most, most).astype(held_as)


def gaussian_with(own_key, extent, spread, bound, shards, heavy, kind=jnp.bfloat16):
    entries = spread * jax.random.normal(own_key, extent, jnp.float32)
    if shards:
        entries = entries * level_of(own_key, extent, shards, -0.22, 0.18)
    return jnp.clip(with_spikes(entries, jax.random.fold_in(own_key, 3), *heavy), -bound, bound).astype(kind)


def setup_inputs(seed: int = 0) -> dict:
    streams_of = jax.random.split(jax.random.key(seed), 6)
    return {
        "queries": noise(streams_of[0], (TOKENS, ATT_WIDTH), 1.0, 6.0, ((0, 32), (1, 4))),
        "keys": noise(streams_of[1], (TOKENS, ATT_WIDTH), 1.0, 6.0, ((0, 32), (1, 4))),
        "values": noise(streams_of[2], (TOKENS, ATT_WIDTH), 1.0, 6.0, ((0, 32), (1, 4))),
        "out_weight": noise(streams_of[3], (D, ATT_WIDTH), ATT_WIDTH ** -0.5, 0.125, ((0, 32), (1, 4))),
        "out_grad": gaussian_with(streams_of[4], (TOKENS, D), 1.0, 6.0, ((0, 32),), (0, 1, 32, 2.75)),
    }


EPSILON = 1e-06
FULL_PRECISION = lax.Precision.HIGHEST

def reference(queries, keys, values, out_weight, out_grad):
    tok_total = queries.shape[0]
    head_cols = queries.shape[1]
    head_count = head_cols // HEAD_DIM
    blk_count = tok_total // BLOCK
    group_cols = head_cols // HEAD_GROUPS
    causal = jnp.tril(jnp.ones((BLOCK, BLOCK), dtype=bool))

    def blocked(array):
        return array.reshape(blk_count, BLOCK, head_count, HEAD_DIM)
    q_blocks = blocked(queries)
    k_blocks = blocked(keys)
    v_blocks = blocked(values)
    kv_state = jnp.einsum('nshe,nshf->nhef', k_blocks.astype(jnp.float32), v_blocks.astype(jnp.float32))
    forward_run = jnp.cumsum(kv_state, axis=0)
    zero_state = jnp.zeros_like(kv_state[:1])
    states = jnp.concatenate([zero_state, forward_run[:-1]], axis=0)
    grad_blocks = out_grad.reshape(blk_count, BLOCK, out_grad.shape[1])

    def masked_scores(q_block, k_block):
        scores = jnp.einsum('the,she->hts', q_block.astype(jnp.float32), k_block.astype(jnp.float32))
        return jnp.where(causal[None], scores, 0.0).astype(jnp.bfloat16)

    def forward(inputs_block):
        q_block, k_block, v_block, state, grad_block = inputs_block
        masked = masked_scores(q_block, k_block)
        attended = jnp.einsum('hts,she->the', masked.astype(jnp.float32), v_block.astype(jnp.float32))
        attended = attended + jnp.einsum('the,hef->thf', q_block.astype(jnp.float32), state, precision=FULL_PRECISION)
        inverse_rms = lax.rsqrt(lax.optimization_barrier(jnp.mean(attended * attended, axis=-1, keepdims=True)) + EPSILON)
        normed = (attended * inverse_rms).astype(jnp.bfloat16).reshape(BLOCK, head_cols)
        partials = []
        for group_idx in range(HEAD_GROUPS):
            lower_col = group_idx * group_cols
            partial_value = lax.dot_general(normed[:, lower_col:lower_col + group_cols], out_weight[:, lower_col:lower_col + group_cols], (((1,), (1,)), ((), ())), preferred_element_type=jnp.float32)
            partials.append(lax.optimization_barrier(partial_value.astype(jnp.bfloat16)).astype(jnp.float32))
        mixed = sum(partials).astype(jnp.bfloat16)
        grad_normed = jnp.dot(grad_block, out_weight, preferred_element_type=jnp.float32).reshape(BLOCK, head_count, HEAD_DIM)
        inner = lax.optimization_barrier(jnp.mean(attended * grad_normed, axis=-1, keepdims=True))
        grad_attended = (inverse_rms * grad_normed - attended * inverse_rms ** 3 * inner).astype(jnp.bfloat16)
        qda_state = jnp.einsum('the,thf->hef', q_block.astype(jnp.float32), grad_attended.astype(jnp.float32))
        return (mixed, normed, grad_attended, qda_state)
    mixed_all, normed_all, grad_att_all, qda_all = lax.map(forward, (q_blocks, k_blocks, v_blocks, states, grad_blocks))
    backward_run = jnp.cumsum(qda_all[::-1], axis=0)[::-1]
    futures = jnp.concatenate([backward_run[1:], zero_state], axis=0)

    def backward(inputs_block):
        q_block, k_block, v_block, state, future, grad_att = inputs_block
        masked = masked_scores(q_block, k_block)
        grad_float = grad_att.astype(jnp.float32)
        dmask = jnp.where(causal[None], jnp.einsum('thf,shf->hts', grad_float, v_block.astype(jnp.float32)), 0.0).astype(jnp.bfloat16)
        grad_q = jnp.einsum('hts,she->the', dmask.astype(jnp.float32), k_block.astype(jnp.float32)) + jnp.einsum('thf,hef->the', grad_float, state, precision=FULL_PRECISION)
        grad_k = jnp.einsum('hts,the->she', dmask.astype(jnp.float32), q_block.astype(jnp.float32)) + jnp.einsum('shf,hef->she', v_block.astype(jnp.float32), future, precision=FULL_PRECISION)
        grad_v = jnp.einsum('hts,thf->shf', masked.astype(jnp.float32), grad_float) + jnp.einsum('she,hef->shf', k_block.astype(jnp.float32), future, precision=FULL_PRECISION)
        return tuple((gradient.astype(jnp.bfloat16).reshape(BLOCK, head_cols) for gradient in (grad_q, grad_k, grad_v)))
    grad_q_all, grad_k_all, grad_v_all = lax.map(backward, (q_blocks, k_blocks, v_blocks, states, futures, grad_att_all))
    grad_weight = lax.dot_general(out_grad, normed_all.reshape(tok_total, head_cols), (((0,), (0,)), ((), ())), preferred_element_type=jnp.float32)
    return (mixed_all.reshape(tok_total, out_grad.shape[1]), grad_q_all.reshape(tok_total, head_cols), grad_k_all.reshape(tok_total, head_cols), grad_v_all.reshape(tok_total, head_cols), grad_weight)
```

```python
import jax
import jax.numpy as jnp
from jax import lax
from jax.experimental import pallas as pl
from jax.experimental.pallas import tpu as pltpu
from jax.sharding import PartitionSpec as P

HEAD_DIM = 128
HEADS = 4
CHUNK = 256
CHUNKS = 4
TOK = 1024
COLS = 512
WIDTH = 4096
EPSILON = 1e-06
MESH = pl.DeviceIdType.MESH
F32 = jnp.float32
BF16 = jnp.bfloat16


def nn(a, b):
    return lax.dot_general(a, b, (((1,), (0,)), ((), ())), preferred_element_type=F32)


def nt(a, b):
    return lax.dot_general(a, b, (((1,), (1,)), ((), ())), preferred_element_type=F32)


def tn(a, b):
    return lax.dot_general(a, b, (((0,), (0,)), ((), ())), preferred_element_type=F32)


def kernel(
    q_hbm, k_hbm, v_hbm, w_hbm, og_hbm,
    mixed_hbm, gq_hbm, gk_hbm, gv_hbm, gw_hbm,
    q, k, v, og, wc, quarter, wr, nb, normed_t, att, nf, inv,
    kvs, states, ga, qdas, futures, own_state, slices, total, totals, offset, before,
    pt, r0, ra, rb, qa, qb, r2a, r2b, mixed, gq, gk, gv, gw,
    load_sem, out_sem,
    wc1_s, wc1_r, wc2_s, wc2_r, wcs_s, wcs_r,
    wq_s, wq_r, wz_s, wz_r, wr1_s, wr1_r, wr2_s, wr2_r, wrs_s, wrs_r,
    sc1_s, sc1_r, sc2_s, sc2_r, sc3_s, sc3_r,
    zs_s, zs_r, zf_s, zf_r,
    rs0_s, rs0_r, rs1_s, rs1_r, rs2_s, rs2_r,
):
    seq = lax.axis_index("seq")
    z = lax.axis_index("head")
    x, y, c = seq // 8, (seq // 2) % 4, seq % 2
    eighth = y * 2 + c

    def at(x_, y_, c_, z_):
        return (x_ * 8 + y_ * 2 + c_, z_)

    def x_dev(d):
        return at((x + d) % 4, y, c, z)

    def y_dev(d):
        return at(x, (y + d) % 4, c, z)

    def z_dev(d):
        return (seq, (z + d) % 4)

    def group_dev(m):
        other = (eighth + m) % 8
        return at(x, other // 2, other % 2, z)

    sibling = at(x, y, 1 - c, z)

    def remote(src, dst, send, recv, device):
        return pltpu.make_async_remote_copy(
            src_ref=src, dst_ref=dst, send_sem=send, recv_sem=recv,
            device_id=device, device_id_type=MESH,
        )

    pending = []

    def go(copies):
        for copy in copies:
            copy.start()
            pending.append(copy)
        return copies

    def arrived(copies):
        for copy in copies:
            copy.wait_recv()

    loads = [
        pltpu.make_async_copy(w_hbm, wc.at[x, y, c], load_sem.at[0]),
        pltpu.make_async_copy(k_hbm, k, load_sem.at[1]),
        pltpu.make_async_copy(v_hbm, v, load_sem.at[2]),
        pltpu.make_async_copy(q_hbm, q, load_sem.at[3]),
        pltpu.make_async_copy(og_hbm, og, load_sem.at[4]),
    ]
    for load in loads:
        load.start()

    barrier = pltpu.get_barrier_semaphore()
    partners = [x_dev(1), x_dev(2), x_dev(3), z_dev(1), z_dev(2), z_dev(3)]
    partners += [group_dev(m) for m in range(1, 8)]
    for partner in partners:
        pl.semaphore_signal(barrier, inc=1, device_id=partner, device_id_type=MESH)
    pl.semaphore_wait(barrier, len(partners))

    loads[0].wait()
    wc_first = go(
        [
            remote(
                wc.at[x, y, c, pl.ds(0, 64)], wc.at[x, y, c, pl.ds(0, 64)],
                wc1_s.at[d - 1], wc1_r.at[d - 1], x_dev(d),
            )
            for d in (1, 3, 2)
        ]
        + [
            remote(
                wc.at[x, y, c, pl.ds(64, 64)], wc.at[x, y, c, pl.ds(64, 64)],
                wc1_s.at[2 + d], wc1_r.at[2 + d], y_dev(d),
            )
            for d in (1, 3, 2)
        ]
    )

    def quarter_rows(part):
        return pl.ds(pl.multiple_of(part * 32, 32), 32)

    quarters = go(
        [
            remote(
                wc.at[x, y, c, quarter_rows((x + d) % 4)], quarter.at[x],
                wq_s.at[d - 1], wq_r.at[d - 1], x_dev(d),
            )
            for d in (1, 3, 2)
        ]
    )
    quarter[x] = wc[x, y, c, quarter_rows(x), :]

    def rows_of(t):
        return pl.ds(pl.multiple_of(t * CHUNK, CHUNK), CHUNK)

    def head_cols(h):
        return slice(h * HEAD_DIM, (h + 1) * HEAD_DIM)

    loads[1].wait()
    loads[2].wait()

    @pl.loop(0, CHUNKS)
    def _(t):
        for h in range(HEADS):
            kvs[t, h] = tn(k[rows_of(t), head_cols(h)], v[rows_of(t), head_cols(h)])

    def publish(n, source):
        for h in range(HEADS):
            state = source[0, h] + source[1, h] + source[2, h] + source[3, h]
            own_state[n, 2 * h] = state[:64].astype(BF16)
            own_state[n, 2 * h + 1] = state[64:].astype(BF16)

    def scan_first(n):
        copies = go(
            [
                remote(
                    own_state.at[n, (eighth + m) % 8], slices.at[n, eighth],
                    sc1_s.at[n, m - 1], sc1_r.at[n, m - 1], group_dev(m),
                )
                for m in range(1, 8)
            ]
        )
        slices[n, eighth] = own_state[n, eighth]
        return copies

    def scan_second(n):
        running = slices[n, 0].astype(F32)
        for i in range(1, 8):
            running = running + slices[n, i].astype(F32)
        total[n] = running.astype(BF16)
        totals[n, x] = total[n]
        return go(
            [
                remote(
                    total.at[n], totals.at[n, x],
                    sc2_s.at[n, d - 1], sc2_r.at[n, d - 1], x_dev(d),
                )
                for d in (1, 3, 2)
            ]
        )

    def scan_third(n):
        base = jnp.zeros((64, HEAD_DIM), F32)
        for i in range(4):
            counts = (x > i) if n == 0 else (x < i)
            base = base + jnp.where(counts, totals[n, i].astype(F32), 0.0)
        order = range(8) if n == 0 else range(7, -1, -1)
        for i in order:
            offset[n, i] = base.astype(BF16)
            base = base + slices[n, i].astype(F32)
        copies = go(
            [
                remote(
                    offset.at[n, (eighth + m) % 8], before.at[n, eighth],
                    sc3_s.at[n, m - 1], sc3_r.at[n, m - 1], group_dev(m),
                )
                for m in range(1, 8)
            ]
        )
        before[n, eighth] = offset[n, eighth]
        return copies

    def incoming(n, h):
        return jnp.concatenate(
            [before[n, 2 * h].astype(F32), before[n, 2 * h + 1].astype(F32)], axis=0
        )

    publish(0, kvs)
    step = scan_first(0)

    row = lax.broadcasted_iota(jnp.int32, (CHUNK, CHUNK), 0)
    col = lax.broadcasted_iota(jnp.int32, (CHUNK, CHUNK), 1)

    def lower(scores):
        return jnp.where(row >= col, scores, 0.0).astype(BF16)

    def upper(scores):
        return jnp.where(row <= col, scores, 0.0).astype(BF16)

    def intra(t):
        for h in range(HEADS):
            qh, kh = q[rows_of(t), head_cols(h)], k[rows_of(t), head_cols(h)]
            att[rows_of(t), head_cols(h)] = nn(lower(nt(qh, kh)), v[rows_of(t), head_cols(h)])

    loads[3].wait()
    pl.loop(0, 2)(intra)
    arrived(step)
    step = scan_second(0)

    arrived(wc_first)
    wc_second = go(
        [
            remote(
                wc.at[:, y, c, pl.ds(0, 64)], wc.at[:, y, c, pl.ds(0, 64)],
                wc2_s.at[d - 1], wc2_r.at[d - 1], y_dev(d),
            )
            for d in (1, 3, 2)
        ]
        + [
            remote(
                wc.at[x, :, c, pl.ds(64, 64)], wc.at[x, :, c, pl.ds(64, 64)],
                wc2_s.at[2 + d], wc2_r.at[2 + d], x_dev(d),
            )
            for d in (1, 3, 2)
        ]
    )
    arrived(quarters)
    to_layer = go(
        [
            remote(
                quarter.at[(z + d) % 4], wr.at[3 - d, y, c, x],
                wz_s.at[d - 1], wz_r.at[d - 1], z_dev(d),
            )
            for d in (1, 3, 2)
        ]
    )

    pl.loop(2, 4)(intra)
    arrived(step)
    step = scan_third(0)
    arrived(to_layer)
    wr_first = go(
        [
            remote(
                wr.at[:, y, c, x, pl.ds(0, 16)], wr.at[:, y, c, x, pl.ds(0, 16)],
                wr1_s.at[d - 1], wr1_r.at[d - 1], x_dev(d),
            )
            for d in (1, 3, 2)
        ]
        + [
            remote(
                wr.at[:, y, c, x, pl.ds(16, 16)], wr.at[:, y, c, x, pl.ds(16, 16)],
                wr1_s.at[2 + d], wr1_r.at[2 + d], y_dev(d),
            )
            for d in (1, 3, 2)
        ]
    )
    arrived(step)

    for h in range(HEADS):
        state = incoming(0, h)
        for t in range(CHUNKS):
            states[t, h] = state.astype(BF16)
            state = state + kvs[t, h]

    def z_send(t, way):
        return remote(
            nb.at[0, rows_of(t)], nb.at[3 if way == 0 else 1, rows_of(t)],
            zs_s.at[way, t], zs_r.at[way, t], z_dev(1 if way == 0 else 3),
        )

    def z_forward(t, way):
        part = pl.ds(pl.multiple_of(t * CHUNK + way * 128, 128), 128)
        return remote(
            nb.at[3 if way == 0 else 1, part], nb.at[2, part],
            zf_s.at[way, t], zf_r.at[way, t], z_dev(1 if way == 0 else 3),
        )

    def forward(t):
        for way in (0, 1):
            z_send(t, way).wait_recv()
            z_forward(t, way).start()

    @pl.loop(0, CHUNKS)
    def _(t):
        for h in range(HEADS):
            a = att[rows_of(t), head_cols(h)] + nn(q[rows_of(t), head_cols(h)], states[t, h])
            scale = lax.rsqrt(jnp.mean(a * a, axis=-1, keepdims=True) + EPSILON)
            n = a * scale
            nf[rows_of(t), head_cols(h)] = n
            inv[rows_of(t), head_cols(h)] = jnp.broadcast_to(scale, n.shape)
            nb[0, rows_of(t), head_cols(h)] = n.astype(BF16)
            normed_t[t, head_cols(h), :] = n.T.astype(BF16)
        for way in (0, 1):
            z_send(t, way).start()

    arrived(wr_first)
    wr_second = go(
        [
            remote(
                wr.at[:, y, c, :, pl.ds(0, 16)], wr.at[:, y, c, :, pl.ds(0, 16)],
                wr2_s.at[d - 1], wr2_r.at[d - 1], y_dev(d),
            )
            for d in (1, 3, 2)
        ]
        + [
            remote(
                wr.at[:, :, c, x, pl.ds(16, 16)], wr.at[:, :, c, x, pl.ds(16, 16)],
                wr2_s.at[2 + d], wr2_r.at[2 + d], x_dev(d),
            )
            for d in (1, 3, 2)
        ]
    )

    def pair_copy(i):
        return remote(
            pt.at[i, 1 - c], r0.at[i], rs0_s.at[i], rs0_r.at[i], sibling
        )

    loads[4].wait()

    @pl.loop(0, 16)
    def _(n):
        i = (x * 4 + 4 + n) % 16
        block = og[:, pl.ds(pl.multiple_of(i * 256, 256), 256)]
        result = nn(normed_t[0], block[:CHUNK])
        for t in range(1, CHUNKS):
            result = result + nn(normed_t[t], block[t * CHUNK:(t + 1) * CHUNK])
        result = result.astype(BF16)
        pt[i, 0] = result[:, :128]
        pt[i, 1] = result[:, 128:]
        pair_copy(i).start()

    arrived(wc_second)
    wc_last = go([remote(wc.at[:, :, c], wc.at[:, :, c], wcs_s.at[0], wcs_r.at[0], sibling)])

    def x_part(d):
        return remote(
            pt.at[pl.ds(pl.multiple_of((x + d) % 4 * 4, 4), 4), c, pl.ds(0, 256)], ra.at[d - 1],
            rs1_s.at[0, d - 1], rs1_r.at[0, d - 1], x_dev(d),
        )

    for d in range(1, 5):
        @pl.loop(0, 4)
        def _(j):
            i = (x + d) % 4 * 4 + j
            pair_copy(i).wait_recv()
            pt[i, c] = (pt[i, c].astype(F32) + r0[i].astype(F32)).astype(BF16)

        if d < 4:
            x_part(d).start()

    def y_part(d, x_):
        return remote(
            pt.at[x_ * 4 + (y + d) % 4, c, pl.ds(256, 256)], rb.at[d - 1, x_],
            rs1_s.at[d, x_], rs1_r.at[d, x_], y_dev(d),
        )

    for d in (1, 3, 2):
        for x_ in range(4):
            y_part(d, x_).start()

    forward(0)

    arrived(wc_last)

    @pl.loop(0, CHUNKS)
    def _(t):
        g_all = nn(og[rows_of(t), :], wc[...].reshape(WIDTH, COLS))
        for h in range(HEADS):
            g = g_all[:, head_cols(h)]
            n = nf[rows_of(t), head_cols(h)]
            inner = jnp.mean(n * g, axis=-1, keepdims=True)
            grad = (inv[rows_of(t), head_cols(h)] * (g - n * inner)).astype(BF16)
            ga[rows_of(t), head_cols(h)] = grad
            qdas[t, h] = tn(q[rows_of(t), head_cols(h)], grad)

    publish(1, qdas)
    step = scan_first(1)
    forward(1)

    for d in range(1, 4):
        x_part(d).wait_recv()
    for j in range(4):
        summed = pt[x * 4 + j, c, :256, :].astype(F32)
        for d in range(3):
            summed = summed + ra[d, j].astype(F32)
        qa[j] = summed.astype(BF16)

    def x_final(d):
        return remote(
            qb.at[(x + d) % 4], r2b.at[d - 1], rs2_s.at[1, d - 1], rs2_r.at[1, d - 1], x_dev(d)
        )

    def y_final(d):
        return remote(
            qa.at[(y + d) % 4], r2a.at[d - 1], rs2_s.at[0, d - 1], rs2_r.at[0, d - 1], y_dev(d)
        )

    finals = go([y_final(d) for d in (1, 3, 2)])
    arrived(step)
    step = scan_second(1)
    for d in range(1, 4):
        for x_ in range(4):
            y_part(d, x_).wait_recv()
    for j in range(4):
        summed = pt[j * 4 + y, c, 256:, :].astype(F32)
        for d in range(3):
            summed = summed + rb[d, j].astype(F32)
        qb[j] = summed.astype(BF16)
    finals += go([x_final(d) for d in (1, 3, 2)])
    arrived(step)
    step = scan_third(1)

    arrived(wr_second)
    wr_last = go([remote(wr.at[:, :, c], wr.at[:, :, c], wrs_s.at[0], wrs_r.at[0], sibling)])
    forward(2)
    arrived(step)

    for h in range(HEADS):
        state = incoming(1, h)
        for t in range(CHUNKS - 1, -1, -1):
            futures[t, h] = state.astype(BF16)
            state = state + qdas[t, h]

    @pl.loop(0, CHUNKS)
    def _(t):
        for h in range(HEADS):
            where = (rows_of(t), head_cols(h))
            qh, kh, vh, gh = q[where], k[where], v[where], ga[where]
            dmask = lower(nt(gh, vh))
            gq[where] = (nn(dmask, kh) + nt(gh, states[t, h])).astype(BF16)
            dmask_t = upper(nt(vh, gh))
            gk[where] = (nn(dmask_t, qh) + nt(vh, futures[t, h])).astype(BF16)
            masked_t = upper(nt(kh, qh))
            gv[where] = (nn(masked_t, gh) + nn(kh, futures[t, h])).astype(BF16)

    stores = [
        pltpu.make_async_copy(gq, gq_hbm, out_sem.at[0]),
        pltpu.make_async_copy(gk, gk_hbm, out_sem.at[1]),
        pltpu.make_async_copy(gv, gv_hbm, out_sem.at[2]),
    ]
    for store in stores:
        store.start()

    forward(3)

    arrived(finals)
    for half, own, others in ((0, qa[y], r2a), (1, qb[x], r2b)):
        summed = own.astype(F32)
        for d in range(3):
            summed = summed + others[d].astype(F32)
        gw[:, half * 256:(half + 1) * 256] = summed.T
    stores.append(pltpu.make_async_copy(gw, gw_hbm, out_sem.at[3]))
    stores[-1].start()

    arrived(wr_last)

    def out_copy(t):
        return pltpu.make_async_copy(
            mixed.at[rows_of(t)], mixed_hbm.at[rows_of(t)], out_sem.at[4 + t]
        )

    @pl.loop(0, CHUNKS)
    def _(t):
        result = nt(nb[0, rows_of(t)], wc[z].reshape(TOK, COLS))
        for d in (1, 3):
            result = result + nt(nb[d, rows_of(t)], wr[d - 1].reshape(TOK, COLS))
        for way in (0, 1):
            z_forward(t, way).wait_recv()
        result = result + nt(nb[2, rows_of(t)], wr[1].reshape(TOK, COLS))
        mixed[rows_of(t), :] = result.astype(BF16)
        out_copy(t).start()

    for copy in pending:
        copy.wait_send()

    @pl.loop(0, CHUNKS)
    def _(t):
        for way in (0, 1):
            z_send(t, way).wait_send()
            z_forward(t, way).wait_send()
        out_copy(t).wait()

    @pl.loop(0, 16)
    def _(i):
        pair_copy(i).wait_send()

    for d in range(1, 4):
        x_part(d).wait_send()
        for x_ in range(4):
            y_part(d, x_).wait_send()
    for store in stores:
        store.wait()


def per_device(queries, keys, values, out_weight, out_grad):
    dma = pltpu.SemaphoreType.DMA
    vm = pltpu.VMEM
    scratch = [
        vm((TOK, COLS), BF16),
        vm((TOK, COLS), BF16),
        vm((TOK, COLS), BF16),
        vm((TOK, WIDTH), BF16),
        vm((4, 4, 2, 128, COLS), BF16),
        vm((4, 32, COLS), BF16),
        vm((3, 4, 2, 4, 32, COLS), BF16),
        vm((4, TOK, COLS), BF16),
        vm((CHUNKS, COLS, CHUNK), BF16),
        vm((TOK, COLS), F32),
        vm((TOK, COLS), F32),
        vm((TOK, COLS), F32),
        vm((CHUNKS, HEADS, 128, 128), F32),
        vm((CHUNKS, HEADS, 128, 128), BF16),
        vm((TOK, COLS), BF16),
        vm((CHUNKS, HEADS, 128, 128), F32),
        vm((CHUNKS, HEADS, 128, 128), BF16),
        vm((2, 8, 64, 128), BF16),
        vm((2, 8, 64, 128), BF16),
        vm((2, 64, 128), BF16),
        vm((2, 4, 64, 128), BF16),
        vm((2, 8, 64, 128), BF16),
        vm((2, 8, 64, 128), BF16),
        vm((16, 2, COLS, 128), BF16),
        vm((16, COLS, 128), BF16),
        vm((3, 4, 256, 128), BF16),
        vm((3, 4, 256, 128), BF16),
        vm((4, 256, 128), BF16),
        vm((4, 256, 128), BF16),
        vm((3, 256, 128), BF16),
        vm((3, 256, 128), BF16),
        vm((TOK, 1024), BF16),
        vm((TOK, COLS), BF16),
        vm((TOK, COLS), BF16),
        vm((TOK, COLS), BF16),
        vm((128, COLS), F32),
        dma((5,)),
        dma((8,)),
    ]
    pairs = [
        (6,), (6,), (1,),
        (3,), (3,), (6,), (6,), (1,),
        (2, 7), (2, 3), (2, 7),
        (2, CHUNKS), (2, CHUNKS),
        (16,), (4, 4), (2, 3),
    ]
    for shape in pairs:
        scratch += [dma(shape), dma(shape)]
    anywhere = pl.BlockSpec(memory_space=pl.ANY)
    return pl.pallas_call(
        kernel,
        out_shape=(
            jax.ShapeDtypeStruct((TOK, 1024), BF16),
            jax.ShapeDtypeStruct((TOK, COLS), BF16),
            jax.ShapeDtypeStruct((TOK, COLS), BF16),
            jax.ShapeDtypeStruct((TOK, COLS), BF16),
            jax.ShapeDtypeStruct((128, COLS), F32),
        ),
        in_specs=[anywhere] * 5,
        out_specs=(anywhere,) * 5,
        scratch_shapes=scratch,
        compiler_params=pltpu.CompilerParams(
            collective_id=0, has_side_effects=True, vmem_limit_bytes=60 << 20
        ),
    )(queries, keys, values, out_weight, out_grad)


def solution(mesh):
    in_specs = (
        P("seq", "head"),
        P("seq", "head"),
        P("seq", "head"),
        P("seq", "head"),
        P("seq", None),
    )
    out_specs = (
        P("seq", "head"),
        P("seq", "head"),
        P("seq", "head"),
        P("seq", "head"),
        P("seq", "head"),
    )
    return jax.shard_map(
        per_device, mesh=mesh, in_specs=in_specs, out_specs=out_specs, check_vma=False
    )
```

```python
import jax
import jax.numpy as jnp
from jax import lax
from jax.experimental import pallas as pl
from jax.experimental.pallas import tpu as pltpu
from jax.sharding import PartitionSpec as P

HEAD_DIM = 128
HEADS = 4
CHUNK = 256
CHUNKS = 4
TOK = 1024
COLS = 512
WIDTH = 4096
EPSILON = 1e-06
MESH = pl.DeviceIdType.MESH
F32 = jnp.float32
BF16 = jnp.bfloat16


def nn(a, b):
    return lax.dot_general(a, b, (((1,), (0,)), ((), ())), preferred_element_type=F32)


def nt(a, b):
    return lax.dot_general(a, b, (((1,), (1,)), ((), ())), preferred_element_type=F32)


def tn(a, b):
    return lax.dot_general(a, b, (((0,), (0,)), ((), ())), preferred_element_type=F32)


def kernel(
    q_hbm, k_hbm, v_hbm, w_hbm, og_hbm,
    mixed_hbm, gq_hbm, gk_hbm, gv_hbm, gw_hbm,
    q, k, v, og, wc, quarter, wr, nb, normed_t, masked_t, att, nf, inv,
    kvs, states, ga, qdas, futures, own_state, peer, chip_state, slices, offset, before, back, final,
    pt, r0, ra, rb, qa, qb, r2a, r2b, acc, mixed, gq, gk, gv, gw,
    load_sem, out_sem,
    wc1_s, wc1_r, wc2_s, wc2_r, wcs_s, wcs_r,
    wq_s, wq_r, wz_s, wz_r, wr1_s, wr1_r, wr2_s, wr2_r, wrs_s, wrs_r,
    sc1_s, sc1_r, sc2_s, sc2_r, sc3_s, sc3_r, sc4_s, sc4_r,
    zs_s, zs_r, zf_s, zf_r,
    rs0_s, rs0_r, rs1_s, rs1_r, rs2_s, rs2_r,
):
    seq = lax.axis_index("seq")
    z = lax.axis_index("head")
    x, y, c = seq // 8, (seq // 2) % 4, seq % 2
    chip = x * 4 + y

    def at(x_, y_, c_, z_):
        return (x_ * 8 + y_ * 2 + c_, z_)

    def x_dev(d):
        return at((x + d) % 4, y, c, z)

    def y_dev(d):
        return at(x, (y + d) % 4, c, z)

    def z_dev(d):
        return (seq, (z + d) % 4)

    def plane_dev(m):
        other = (chip + m) % 16
        return at(other // 4, other % 4, c, z)

    sibling = at(x, y, 1 - c, z)

    def remote(src, dst, send, recv, device):
        return pltpu.make_async_remote_copy(
            src_ref=src, dst_ref=dst, send_sem=send, recv_sem=recv,
            device_id=device, device_id_type=MESH,
        )

    pending = []

    def go(copies):
        for copy in copies:
            copy.start()
            pending.append(copy)
        return copies

    def arrived(copies):
        for copy in copies:
            copy.wait_recv()

    loads = [
        pltpu.make_async_copy(w_hbm, wc.at[x, y, c], load_sem.at[0]),
        pltpu.make_async_copy(k_hbm, k, load_sem.at[1]),
        pltpu.make_async_copy(v_hbm, v, load_sem.at[2]),
        pltpu.make_async_copy(q_hbm, q, load_sem.at[3]),
        pltpu.make_async_copy(og_hbm, og, load_sem.at[4]),
    ]
    for load in loads[:4]:
        load.start()

    barrier = pltpu.get_barrier_semaphore()
    partners = [plane_dev(m) for m in range(1, 16)] + [sibling, z_dev(1), z_dev(2), z_dev(3)]
    for partner in partners:
        pl.semaphore_signal(barrier, inc=1, device_id=partner, device_id_type=MESH)

    def rows_of(t):
        return pl.ds(pl.multiple_of(t * CHUNK, CHUNK), CHUNK)

    def head_cols(h):
        return slice(h * HEAD_DIM, (h + 1) * HEAD_DIM)

    loads[1].wait()
    loads[2].wait()
    loads[3].wait()
    loads[4].start()

    @pl.loop(0, CHUNKS)
    def _(t):
        for h in range(HEADS):
            kvs[t, h] = tn(k[rows_of(t), head_cols(h)], v[rows_of(t), head_cols(h)])

    def publish(n, source):
        for h in range(HEADS):
            state = source[0, h] + source[1, h] + source[2, h] + source[3, h]
            own_state[n, h // 2, (h % 2) * 8:(h % 2) * 8 + 8] = (
                state.astype(BF16).reshape(8, 16, HEAD_DIM)
            )

    def scan_first(n):
        return go(
            [remote(own_state.at[n, 1 - c], peer.at[n], sc1_s.at[n, 0], sc1_r.at[n, 0], sibling)]
        )

    def scan_second(n):
        chip_state[n] = (own_state[n, c].astype(F32) + peer[n].astype(F32)).astype(BF16)
        for m in range(1, 16):
            remote(
                chip_state.at[n, (chip + m) % 16], slices.at[n, chip],
                sc2_s.at[n], sc2_r.at[n], plane_dev(m),
            ).start()
        whole = remote(
            chip_state.at[n, pl.ds(0, 15)], slices.at[n, pl.ds(0, 15)],
            sc2_s.at[n], sc2_r.at[n], plane_dev(1),
        )
        pending.append(whole)
        slices[n, chip] = chip_state[n, chip]
        return [whole]

    def scan_third(n):
        base = jnp.zeros((16, HEAD_DIM), F32)
        for i in range(16) if n == 0 else range(15, -1, -1):
            offset[n, i] = base.astype(BF16)
            base = base + slices[n, i].astype(F32)
        for m in range(1, 16):
            remote(
                offset.at[n, (chip + m) % 16], before.at[n, chip],
                sc3_s.at[n], sc3_r.at[n], plane_dev(m),
            ).start()
        whole = remote(
            offset.at[n, pl.ds(0, 15)], before.at[n, pl.ds(0, 15)],
            sc3_s.at[n], sc3_r.at[n], plane_dev(1),
        )
        pending.append(whole)
        before[n, chip] = offset[n, chip]
        return [whole]

    def scan_fourth(n):
        base = before[n].astype(F32)
        self_second, other_second = (c == 1, c == 0) if n == 0 else (c == 0, c == 1)
        back[n] = (base + jnp.where(other_second, own_state[n, c].astype(F32), 0.0)).astype(BF16)
        copies = go(
            [remote(back.at[n], final.at[n, c], sc4_s.at[n, 0], sc4_r.at[n, 0], sibling)]
        )
        final[n, c] = (base + jnp.where(self_second, peer[n].astype(F32), 0.0)).astype(BF16)
        return copies

    def incoming(n, h):
        half = final[n, h // 2, (h % 2) * 8:(h % 2) * 8 + 8].astype(F32)
        return half.reshape(HEAD_DIM, HEAD_DIM)

    publish(0, kvs)
    pl.semaphore_wait(barrier, len(partners))
    step = scan_first(0)

    loads[0].wait()
    wc_first = go(
        [
            remote(
                wc.at[x, y, c, pl.ds(0, 64)], wc.at[x, y, c, pl.ds(0, 64)],
                wc1_s.at[d - 1], wc1_r.at[d - 1], x_dev(d),
            )
            for d in (1, 3, 2)
        ]
        + [
            remote(
                wc.at[x, y, c, pl.ds(64, 64)], wc.at[x, y, c, pl.ds(64, 64)],
                wc1_s.at[2 + d], wc1_r.at[2 + d], y_dev(d),
            )
            for d in (1, 3, 2)
        ]
    )

    def quarter_rows(part):
        return pl.ds(pl.multiple_of(part * 32, 32), 32)

    quarters = go(
        [
            remote(
                wc.at[x, y, c, quarter_rows((x + d) % 4)], quarter.at[x],
                wq_s.at[d - 1], wq_r.at[d - 1], x_dev(d),
            )
            for d in (1, 3, 2)
        ]
    )
    quarter[x] = wc[x, y, c, quarter_rows(x), :]

    row = lax.broadcasted_iota(jnp.int32, (CHUNK, CHUNK), 0)
    col = lax.broadcasted_iota(jnp.int32, (CHUNK, CHUNK), 1)

    def lower(scores):
        return jnp.where(row >= col, scores, 0.0).astype(BF16)

    def upper(scores):
        return jnp.where(row <= col, scores, 0.0).astype(BF16)

    def intra(t):
        for h in range(HEADS):
            qh, kh = q[rows_of(t), head_cols(h)], k[rows_of(t), head_cols(h)]
            att[rows_of(t), head_cols(h)] = nn(lower(nt(qh, kh)), v[rows_of(t), head_cols(h)])

    pl.loop(0, 1)(intra)
    arrived(step)
    step = scan_second(0)
    pl.loop(1, CHUNKS)(intra)
    arrived(step)
    step = scan_third(0)
    arrived(wc_first)
    arrived(quarters)

    wc_second = go(
        [
            remote(
                wc.at[:, y, c, pl.ds(0, 64)], wc.at[:, y, c, pl.ds(0, 64)],
                wc2_s.at[d - 1], wc2_r.at[d - 1], y_dev(d),
            )
            for d in (1, 3, 2)
        ]
        + [
            remote(
                wc.at[x, :, c, pl.ds(64, 64)], wc.at[x, :, c, pl.ds(64, 64)],
                wc2_s.at[2 + d], wc2_r.at[2 + d], x_dev(d),
            )
            for d in (1, 3, 2)
        ]
    )

    to_layer = go(
        [
            remote(
                quarter.at[(z + d) % 4], wr.at[3 - d, y, c, x],
                wz_s.at[d - 1], wz_r.at[d - 1], z_dev(d),
            )
            for d in (1, 3, 2)
        ]
    )

    @pl.loop(0, CHUNKS)
    def _(t):
        for h in range(HEADS):
            masked_t[t, h] = upper(nt(k[rows_of(t), head_cols(h)], q[rows_of(t), head_cols(h)]))

    arrived(step)
    step = scan_fourth(0)
    arrived(step)

    for h in range(HEADS):
        state = incoming(0, h)
        for t in range(CHUNKS):
            states[t, h] = state.astype(BF16)
            state = state + kvs[t, h]

    def z_send(t, way):
        return remote(
            nb.at[0, rows_of(t)], nb.at[3 if way == 0 else 1, rows_of(t)],
            zs_s.at[way, t], zs_r.at[way, t], z_dev(1 if way == 0 else 3),
        )

    def z_forward(t, way):
        part = pl.ds(pl.multiple_of(t * CHUNK + way * 128, 128), 128)
        return remote(
            nb.at[3 if way == 0 else 1, part], nb.at[2, part],
            zf_s.at[way, t], zf_r.at[way, t], z_dev(1 if way == 0 else 3),
        )

    def forward(t):
        for way in (0, 1):
            z_send(t, way).wait_recv()
            z_forward(t, way).start()

    @pl.loop(0, CHUNKS)
    def _(t):
        for h in range(HEADS):
            a = att[rows_of(t), head_cols(h)] + nn(q[rows_of(t), head_cols(h)], states[t, h])
            scale = lax.rsqrt(jnp.mean(a * a, axis=-1, keepdims=True) + EPSILON)
            n = a * scale
            nf[rows_of(t), head_cols(h)] = n
            inv[rows_of(t), head_cols(h)] = jnp.broadcast_to(scale, n.shape)
            nb[0, rows_of(t), head_cols(h)] = n.astype(BF16)
            normed_t[head_cols(h), rows_of(t)] = n.T.astype(BF16)
        for way in (0, 1):
            z_send(t, way).start()

    arrived(to_layer)
    wr_first = go(
        [
            remote(
                wr.at[:, y, c, x, pl.ds(0, 16)], wr.at[:, y, c, x, pl.ds(0, 16)],
                wr1_s.at[d - 1], wr1_r.at[d - 1], x_dev(d),
            )
            for d in (1, 3, 2)
        ]
        + [
            remote(
                wr.at[:, y, c, x, pl.ds(16, 16)], wr.at[:, y, c, x, pl.ds(16, 16)],
                wr1_s.at[2 + d], wr1_r.at[2 + d], y_dev(d),
            )
            for d in (1, 3, 2)
        ]
    )

    def pair_copy(i):
        return remote(
            pt.at[i, :, 1 - c], r0.at[i], rs0_s.at[i], rs0_r.at[i], sibling
        )

    loads[4].wait()

    def term(i, two):
        block = og[:, pl.ds(pl.multiple_of((i * 2 + two) * 512, 512), 512)]
        result = nn(normed_t[...], block).astype(BF16)
        for n in range(4):
            pt[i, two * 2 + n // 2, n % 2] = result[:, n * 128:(n + 1) * 128]

    def terms(d):
        i = (x + d) % 4
        pl.loop(0, 2)(lambda two: term(i, two))
        pair_copy(i).start()

    terms(1)
    terms(2)
    arrived(wc_second)
    wc_last = go([remote(wc.at[:, :, c], wc.at[:, :, c], wcs_s.at[0], wcs_r.at[0], sibling)])

    arrived(wr_first)
    wr_second = go(
        [
            remote(
                wr.at[:, y, c, :, pl.ds(0, 16)], wr.at[:, y, c, :, pl.ds(0, 16)],
                wr2_s.at[d - 1], wr2_r.at[d - 1], y_dev(d),
            )
            for d in (1, 3, 2)
        ]
        + [
            remote(
                wr.at[:, :, c, x, pl.ds(16, 16)], wr.at[:, :, c, x, pl.ds(16, 16)],
                wr2_s.at[2 + d], wr2_r.at[2 + d], x_dev(d),
            )
            for d in (1, 3, 2)
        ]
    )

    terms(3)

    arrived(wc_last)

    @pl.loop(0, 2)
    def _(two):
        both = pl.ds(pl.multiple_of(two * 512, 512), 512)
        g_all = nn(og[both, :], wc[...].reshape(WIDTH, COLS))
        for part in range(2):
            t = two * 2 + part
            for h in range(HEADS):
                g = g_all[part * CHUNK:(part + 1) * CHUNK, head_cols(h)]
                n = nf[rows_of(t), head_cols(h)]
                inner = jnp.mean(n * g, axis=-1, keepdims=True)
                grad = (inv[rows_of(t), head_cols(h)] * (g - n * inner)).astype(BF16)
                ga[rows_of(t), head_cols(h)] = grad
                qdas[t, h] = tn(q[rows_of(t), head_cols(h)], grad)

    publish(1, qdas)
    step = scan_first(1)
    forward(0)
    forward(1)

    def inner_gradients(t):
        for h in range(HEADS):
            where = (rows_of(t), head_cols(h))
            qh, kh, vh, gh = q[where], k[where], v[where], ga[where]
            dmask = lower(nt(gh, vh))
            gq[where] = (nn(dmask, kh) + nt(gh, states[t, h])).astype(BF16)
            dmask_t = upper(nt(vh, gh))
            att[where] = nn(dmask_t, qh)
            nf[where] = nn(masked_t[t, h], gh)

    def x_final(d):
        return remote(
            qb.at[(x + d) % 4], r2b.at[d - 1], rs2_s.at[1, d - 1], rs2_r.at[1, d - 1], x_dev(d)
        )

    def y_final(d):
        return remote(
            qa.at[(y + d) % 4], r2a.at[d - 1], rs2_s.at[0, d - 1], rs2_r.at[0, d - 1], y_dev(d)
        )

    terms(0)
    arrived(step)
    step = scan_second(1)
    pl.loop(0, 3)(inner_gradients)
    arrived(step)
    step = scan_third(1)

    def x_part(d):
        return remote(
            pt.at[(x + d) % 4, :, c, pl.ds(0, 256)], ra.at[d - 1],
            rs1_s.at[0, d - 1], rs1_r.at[0, d - 1], x_dev(d),
        )

    for d in range(1, 5):
        i = (x + d) % 4
        pair_copy(i).wait_recv()

        @pl.loop(0, 4)
        def _(j):
            pt[i, j, c] = (pt[i, j, c].astype(F32) + r0[i, j].astype(F32)).astype(BF16)

        if d < 4:
            x_part(d).start()

    def y_part(d):
        return remote(
            pt.at[:, (y + d) % 4, c, pl.ds(256, 256)], rb.at[d - 1],
            rs1_s.at[1, d - 1], rs1_r.at[1, d - 1], y_dev(d),
        )

    for d in (1, 3, 2):
        y_part(d).start()

    pl.loop(3, CHUNKS)(inner_gradients)
    forward(2)
    forward(3)
    arrived(wr_second)
    wr_last = go([remote(wr.at[:, :, c], wr.at[:, :, c], wrs_s.at[0], wrs_r.at[0], sibling)])
    arrived(step)
    step = scan_fourth(1)
    arrived(step)

    for h in range(HEADS):
        state = incoming(1, h)
        for t in range(CHUNKS - 1, -1, -1):
            futures[t, h] = state.astype(BF16)
            state = state + qdas[t, h]

    @pl.loop(0, CHUNKS)
    def _(t):
        for h in range(HEADS):
            where = (rows_of(t), head_cols(h))
            gk[where] = (att[where] + nt(v[where], futures[t, h])).astype(BF16)
            gv[where] = (nf[where] + nn(k[where], futures[t, h])).astype(BF16)

    stores = [
        pltpu.make_async_copy(gq, gq_hbm, out_sem.at[0]),
        pltpu.make_async_copy(gk, gk_hbm, out_sem.at[1]),
        pltpu.make_async_copy(gv, gv_hbm, out_sem.at[2]),
    ]
    for store in stores:
        store.start()

    arrived(wr_last)

    @pl.loop(0, 2)
    def _(two):
        both = pl.ds(pl.multiple_of(two * 512, 512), 512)
        result = nt(nb[0, both], wc[z].reshape(TOK, COLS))
        for d in (1, 3):
            result = result + nt(nb[d, both], wr[d - 1].reshape(TOK, COLS))
        acc[both, :] = result

    for d in range(1, 4):
        x_part(d).wait_recv()
    for j in range(4):
        summed = pt[x, j, c, :256, :].astype(F32)
        for d in range(3):
            summed = summed + ra[d, j].astype(F32)
        qa[j] = summed.astype(BF16)

    finals = go([y_final(d) for d in (1, 3, 2)])
    for d in range(1, 4):
        y_part(d).wait_recv()
    for j in range(4):
        summed = pt[j, y, c, 256:, :].astype(F32)
        for d in range(3):
            summed = summed + rb[d, j].astype(F32)
        qb[j] = summed.astype(BF16)
    finals += go([x_final(d) for d in (1, 3, 2)])
    def out_copy(t):
        return pltpu.make_async_copy(
            mixed.at[rows_of(t)], mixed_hbm.at[rows_of(t)], out_sem.at[4 + t]
        )

    @pl.loop(0, CHUNKS)
    def _(t):
        for way in (0, 1):
            z_forward(t, way).wait_recv()
        result = acc[rows_of(t), :] + nt(nb[2, rows_of(t)], wr[1].reshape(TOK, COLS))
        mixed[rows_of(t), :] = result.astype(BF16)
        out_copy(t).start()

    arrived(finals)
    for half, own, others in ((0, qa[y], r2a), (1, qb[x], r2b)):
        summed = own.astype(F32)
        for d in range(3):
            summed = summed + others[d].astype(F32)
        gw[:, half * 256:(half + 1) * 256] = summed.T
    stores.append(pltpu.make_async_copy(gw, gw_hbm, out_sem.at[3]))
    stores[-1].start()

    for copy in pending:
        copy.wait_send()

    @pl.loop(0, CHUNKS)
    def _(t):
        for way in (0, 1):
            z_send(t, way).wait_send()
            z_forward(t, way).wait_send()
        out_copy(t).wait()

    for i in range(4):
        pair_copy(i).wait_send()

    for d in range(1, 4):
        x_part(d).wait_send()
        y_part(d).wait_send()
    for store in stores:
        store.wait()


def deliver(*refs):
    sources, targets, held = refs[:5], refs[5:10], refs[10:15]
    in_sem, out_sem = refs[15:]
    pieces = []
    for a, source in enumerate(sources):
        rows = source.shape[0] // 4
        for part in range(4):
            at = pl.ds(part * rows, rows)
            n = a * 4 + part
            pieces.append(
                (
                    pltpu.make_async_copy(source.at[at], held[a].at[at], in_sem.at[n]),
                    pltpu.make_async_copy(held[a].at[at], targets[a].at[at], out_sem.at[n]),
                )
            )
    for load, _ in pieces:
        load.start()
    for load, store in pieces:
        load.wait()
        store.start()
    for _, store in pieces:
        store.wait()


def per_device(queries, keys, values, out_weight, out_grad):
    dma = pltpu.SemaphoreType.DMA
    vm = pltpu.VMEM
    scratch = [
        vm((TOK, COLS), BF16),
        vm((TOK, COLS), BF16),
        vm((TOK, COLS), BF16),
        vm((TOK, WIDTH), BF16),
        vm((4, 4, 2, 128, COLS), BF16),
        vm((4, 32, COLS), BF16),
        vm((3, 4, 2, 4, 32, COLS), BF16),
        vm((4, TOK, COLS), BF16),
        vm((COLS, TOK), BF16),
        vm((CHUNKS, HEADS, CHUNK, CHUNK), BF16),
        vm((TOK, COLS), F32),
        vm((TOK, COLS), F32),
        vm((TOK, COLS), F32),
        vm((CHUNKS, HEADS, 128, 128), F32),
        vm((CHUNKS, HEADS, 128, 128), BF16),
        vm((TOK, COLS), BF16),
        vm((CHUNKS, HEADS, 128, 128), F32),
        vm((CHUNKS, HEADS, 128, 128), BF16),
        vm((2, 2, 16, 16, 128), BF16),
        vm((2, 16, 16, 128), BF16),
        vm((2, 16, 16, 128), BF16),
        vm((2, 16, 16, 128), BF16),
        vm((2, 16, 16, 128), BF16),
        vm((2, 16, 16, 128), BF16),
        vm((2, 16, 16, 128), BF16),
        vm((2, 2, 16, 16, 128), BF16),
        vm((4, 4, 2, COLS, 128), BF16),
        vm((4, 4, COLS, 128), BF16),
        vm((3, 4, 256, 128), BF16),
        vm((3, 4, 256, 128), BF16),
        vm((4, 256, 128), BF16),
        vm((4, 256, 128), BF16),
        vm((3, 256, 128), BF16),
        vm((3, 256, 128), BF16),
        vm((TOK, 1024), F32),
        vm((TOK, 1024), BF16),
        vm((TOK, COLS), BF16),
        vm((TOK, COLS), BF16),
        vm((TOK, COLS), BF16),
        vm((128, COLS), F32),
        dma((5,)),
        dma((8,)),
    ]
    pairs = [
        (6,), (6,), (1,),
        (3,), (3,), (6,), (6,), (1,),
        (2, 1), (2,), (2,), (2, 1),
        (2, CHUNKS), (2, CHUNKS),
        (4,), (2, 3), (2, 3),
    ]
    for shape in pairs:
        scratch += [dma(shape), dma(shape)]
    anywhere = pl.BlockSpec(memory_space=pl.ANY)
    shapes = (
        jax.ShapeDtypeStruct((TOK, 1024), BF16),
        jax.ShapeDtypeStruct((TOK, COLS), BF16),
        jax.ShapeDtypeStruct((TOK, COLS), BF16),
        jax.ShapeDtypeStruct((TOK, COLS), BF16),
        jax.ShapeDtypeStruct((128, COLS), F32),
    )
    results = pl.pallas_call(
        kernel,
        out_shape=shapes,
        in_specs=[anywhere] * 5,
        out_specs=(anywhere,) * 5,
        scratch_shapes=scratch,
        compiler_params=pltpu.CompilerParams(
            collective_id=0, has_side_effects=True, vmem_limit_bytes=60 << 20
        ),
    )(queries, keys, values, out_weight, out_grad)
    return pl.pallas_call(
        deliver,
        out_shape=shapes,
        in_specs=[anywhere] * 5,
        out_specs=(anywhere,) * 5,
        scratch_shapes=[vm(shape.shape, shape.dtype) for shape in shapes] + [dma((20,)), dma((20,))],
        compiler_params=pltpu.CompilerParams(vmem_limit_bytes=60 << 20),
    )(*results)


def solution(mesh):
    in_specs = (
        P("seq", "head"),
        P("seq", "head"),
        P("seq", "head"),
        P("seq", "head"),
        P("seq", None),
    )
    out_specs = (
        P("seq", "head"),
        P("seq", "head"),
        P("seq", "head"),
        P("seq", "head"),
        P("seq", "head"),
    )
    return jax.shard_map(
        per_device, mesh=mesh, in_specs=in_specs, out_specs=out_specs, check_vma=False
    )
```

```python
import jax
import jax.numpy as jnp
from jax import lax
from jax.experimental import pallas as pl
from jax.experimental.pallas import tpu as pltpu
from jax.sharding import PartitionSpec as P

HEAD_DIM = 128
HEADS = 4
CHUNK = 256
CHUNKS = 4
TOK = 1024
COLS = 512
WIDTH = 4096
EPSILON = 1e-06
MESH = pl.DeviceIdType.MESH
F32 = jnp.float32
BF16 = jnp.bfloat16


def nn(a, b):
    return lax.dot_general(a, b, (((1,), (0,)), ((), ())), preferred_element_type=F32)


def nt(a, b):
    return lax.dot_general(a, b, (((1,), (1,)), ((), ())), preferred_element_type=F32)


def tn(a, b):
    return lax.dot_general(a, b, (((0,), (0,)), ((), ())), preferred_element_type=F32)


def kernel(
    q_hbm, k_hbm, v_hbm, w_hbm, og_hbm,
    mixed, gq, gk, gv, gw,
    q, k, v, og, wc, quarter, wr, nb, normed_t, masked_t, att, nf, inv,
    kvs, states, ga, qdas, futures, own_state, peer, chip_state, slices, offset, before, back, final,
    pt, r0, ra, rb, qa, qb, r2a, r2b, acc,
    load_sem,
    wc1_s, wc1_r, wc2_s, wc2_r, wcs_s, wcs_r,
    wq_s, wq_r, wz_s, wz_r, wr1_s, wr1_r, wr2_s, wr2_r, wrs_s, wrs_r,
    sc1_s, sc1_r, sc2_s, sc2_r, sc3_s, sc3_r, sc4_s, sc4_r,
    zs_s, zs_r, zf_s, zf_r,
    rs0_s, rs0_r, rs1_s, rs1_r, rs2_s, rs2_r,
):
    seq = lax.axis_index("seq")
    z = lax.axis_index("head")
    x, y, c = seq // 8, (seq // 2) % 4, seq % 2
    chip = x * 4 + y

    def at(x_, y_, c_, z_):
        return (x_ * 8 + y_ * 2 + c_, z_)

    def x_dev(d):
        return at((x + d) % 4, y, c, z)

    def y_dev(d):
        return at(x, (y + d) % 4, c, z)

    def z_dev(d):
        return (seq, (z + d) % 4)

    def plane_dev(m):
        other = (chip + m) % 16
        return at(other // 4, other % 4, c, z)

    sibling = at(x, y, 1 - c, z)

    def remote(src, dst, send, recv, device):
        return pltpu.make_async_remote_copy(
            src_ref=src, dst_ref=dst, send_sem=send, recv_sem=recv,
            device_id=device, device_id_type=MESH,
        )

    pending = []

    def go(copies):
        for copy in copies:
            copy.start()
            pending.append(copy)
        return copies

    def arrived(copies):
        for copy in copies:
            copy.wait_recv()

    loads = [
        pltpu.make_async_copy(w_hbm, wc.at[x, y, c], load_sem.at[0]),
        pltpu.make_async_copy(k_hbm, k, load_sem.at[1]),
        pltpu.make_async_copy(v_hbm, v, load_sem.at[2]),
        pltpu.make_async_copy(q_hbm, q, load_sem.at[3]),
        pltpu.make_async_copy(og_hbm, og, load_sem.at[4]),
    ]
    for load in loads[:4]:
        load.start()

    barrier = pltpu.get_barrier_semaphore()
    partners = [plane_dev(m) for m in range(1, 16)] + [sibling, z_dev(1), z_dev(2), z_dev(3)]
    for partner in partners:
        pl.semaphore_signal(barrier, inc=1, device_id=partner, device_id_type=MESH)

    def rows_of(t):
        return pl.ds(pl.multiple_of(t * CHUNK, CHUNK), CHUNK)

    def head_cols(h):
        return slice(h * HEAD_DIM, (h + 1) * HEAD_DIM)

    loads[1].wait()
    loads[2].wait()
    loads[3].wait()
    loads[4].start()

    @pl.loop(0, CHUNKS)
    def _(t):
        for h in range(HEADS):
            kvs[t, h] = tn(k[rows_of(t), head_cols(h)], v[rows_of(t), head_cols(h)])

    def publish(n, source):
        for h in range(HEADS):
            state = source[0, h] + source[1, h] + source[2, h] + source[3, h]
            own_state[n, h // 2, (h % 2) * 8:(h % 2) * 8 + 8] = (
                state.astype(BF16).reshape(8, 16, HEAD_DIM)
            )

    def scan_first(n):
        return go(
            [remote(own_state.at[n, 1 - c], peer.at[n], sc1_s.at[n, 0], sc1_r.at[n, 0], sibling)]
        )

    def scan_second(n):
        chip_state[n] = (own_state[n, c].astype(F32) + peer[n].astype(F32)).astype(BF16)
        for m in range(1, 16):
            remote(
                chip_state.at[n, (chip + m) % 16], slices.at[n, chip],
                sc2_s.at[n], sc2_r.at[n], plane_dev(m),
            ).start()
        whole = remote(
            chip_state.at[n, pl.ds(0, 15)], slices.at[n, pl.ds(0, 15)],
            sc2_s.at[n], sc2_r.at[n], plane_dev(1),
        )
        pending.append(whole)
        slices[n, chip] = chip_state[n, chip]
        return [whole]

    def scan_third(n):
        base = jnp.zeros((16, HEAD_DIM), F32)
        for i in range(16) if n == 0 else range(15, -1, -1):
            offset[n, i] = base.astype(BF16)
            base = base + slices[n, i].astype(F32)
        for m in range(1, 16):
            remote(
                offset.at[n, (chip + m) % 16], before.at[n, chip],
                sc3_s.at[n], sc3_r.at[n], plane_dev(m),
            ).start()
        whole = remote(
            offset.at[n, pl.ds(0, 15)], before.at[n, pl.ds(0, 15)],
            sc3_s.at[n], sc3_r.at[n], plane_dev(1),
        )
        pending.append(whole)
        before[n, chip] = offset[n, chip]
        return [whole]

    def scan_fourth(n):
        base = before[n].astype(F32)
        self_second, other_second = (c == 1, c == 0) if n == 0 else (c == 0, c == 1)
        back[n] = (base + jnp.where(other_second, own_state[n, c].astype(F32), 0.0)).astype(BF16)
        copies = go(
            [remote(back.at[n], final.at[n, c], sc4_s.at[n, 0], sc4_r.at[n, 0], sibling)]
        )
        final[n, c] = (base + jnp.where(self_second, peer[n].astype(F32), 0.0)).astype(BF16)
        return copies

    def incoming(n, h):
        half = final[n, h // 2, (h % 2) * 8:(h % 2) * 8 + 8].astype(F32)
        return half.reshape(HEAD_DIM, HEAD_DIM)

    publish(0, kvs)
    pl.semaphore_wait(barrier, len(partners))
    step = scan_first(0)

    loads[0].wait()
    wc_first = go(
        [
            remote(
                wc.at[x, y, c, pl.ds(0, 64)], wc.at[x, y, c, pl.ds(0, 64)],
                wc1_s.at[d - 1], wc1_r.at[d - 1], x_dev(d),
            )
            for d in (1, 3, 2)
        ]
        + [
            remote(
                wc.at[x, y, c, pl.ds(64, 64)], wc.at[x, y, c, pl.ds(64, 64)],
                wc1_s.at[2 + d], wc1_r.at[2 + d], y_dev(d),
            )
            for d in (1, 3, 2)
        ]
    )

    def quarter_rows(part):
        return pl.ds(pl.multiple_of(part * 32, 32), 32)

    quarters = go(
        [
            remote(
                wc.at[x, y, c, quarter_rows((x + d) % 4)], quarter.at[x],
                wq_s.at[d - 1], wq_r.at[d - 1], x_dev(d),
            )
            for d in (1, 3, 2)
        ]
    )
    quarter[x] = wc[x, y, c, quarter_rows(x), :]

    row = lax.broadcasted_iota(jnp.int32, (CHUNK, CHUNK), 0)
    col = lax.broadcasted_iota(jnp.int32, (CHUNK, CHUNK), 1)

    def lower(scores):
        return jnp.where(row >= col, scores, 0.0).astype(BF16)

    def upper(scores):
        return jnp.where(row <= col, scores, 0.0).astype(BF16)

    def intra(t):
        for h in range(HEADS):
            qh, kh = q[rows_of(t), head_cols(h)], k[rows_of(t), head_cols(h)]
            att[rows_of(t), head_cols(h)] = nn(lower(nt(qh, kh)), v[rows_of(t), head_cols(h)])

    pl.loop(0, 1)(intra)
    arrived(step)
    step = scan_second(0)
    pl.loop(1, CHUNKS)(intra)
    arrived(step)
    step = scan_third(0)
    arrived(wc_first)
    arrived(quarters)

    wc_second = go(
        [
            remote(
                wc.at[:, y, c, pl.ds(0, 64)], wc.at[:, y, c, pl.ds(0, 64)],
                wc2_s.at[d - 1], wc2_r.at[d - 1], y_dev(d),
            )
            for d in (1, 3, 2)
        ]
        + [
            remote(
                wc.at[x, :, c, pl.ds(64, 64)], wc.at[x, :, c, pl.ds(64, 64)],
                wc2_s.at[2 + d], wc2_r.at[2 + d], x_dev(d),
            )
            for d in (1, 3, 2)
        ]
    )

    to_layer = go(
        [
            remote(
                quarter.at[(z + d) % 4], wr.at[3 - d, y, c, x],
                wz_s.at[d - 1], wz_r.at[d - 1], z_dev(d),
            )
            for d in (1, 3, 2)
        ]
    )

    @pl.loop(0, CHUNKS)
    def _(t):
        for h in range(HEADS):
            masked_t[t, h] = upper(nt(k[rows_of(t), head_cols(h)], q[rows_of(t), head_cols(h)]))

    arrived(step)
    step = scan_fourth(0)
    arrived(step)

    for h in range(HEADS):
        state = incoming(0, h)
        for t in range(CHUNKS):
            states[t, h] = state.astype(BF16)
            state = state + kvs[t, h]

    def z_send(t, way):
        return remote(
            nb.at[0, rows_of(t)], nb.at[3 if way == 0 else 1, rows_of(t)],
            zs_s.at[way, t], zs_r.at[way, t], z_dev(1 if way == 0 else 3),
        )

    def z_forward(t, way):
        part = pl.ds(pl.multiple_of(t * CHUNK + way * 128, 128), 128)
        return remote(
            nb.at[3 if way == 0 else 1, part], nb.at[2, part],
            zf_s.at[way, t], zf_r.at[way, t], z_dev(1 if way == 0 else 3),
        )

    def forward(t):
        for way in (0, 1):
            z_send(t, way).wait_recv()
            z_forward(t, way).start()

    @pl.loop(0, CHUNKS)
    def _(t):
        for h in range(HEADS):
            a = att[rows_of(t), head_cols(h)] + nn(q[rows_of(t), head_cols(h)], states[t, h])
            scale = lax.rsqrt(jnp.mean(a * a, axis=-1, keepdims=True) + EPSILON)
            n = a * scale
            nf[rows_of(t), head_cols(h)] = n
            inv[rows_of(t), head_cols(h)] = jnp.broadcast_to(scale, n.shape)
            nb[0, rows_of(t), head_cols(h)] = n.astype(BF16)
            normed_t[head_cols(h), rows_of(t)] = n.T.astype(BF16)
        for way in (0, 1):
            z_send(t, way).start()

    arrived(to_layer)
    wr_first = go(
        [
            remote(
                wr.at[:, y, c, x, pl.ds(0, 16)], wr.at[:, y, c, x, pl.ds(0, 16)],
                wr1_s.at[d - 1], wr1_r.at[d - 1], x_dev(d),
            )
            for d in (1, 3, 2)
        ]
        + [
            remote(
                wr.at[:, y, c, x, pl.ds(16, 16)], wr.at[:, y, c, x, pl.ds(16, 16)],
                wr1_s.at[2 + d], wr1_r.at[2 + d], y_dev(d),
            )
            for d in (1, 3, 2)
        ]
    )

    def pair_copy(i):
        return remote(
            pt.at[i, :, 1 - c], r0.at[i], rs0_s.at[i], rs0_r.at[i], sibling
        )

    loads[4].wait()

    def term(i, two):
        block = og[:, pl.ds(pl.multiple_of((i * 2 + two) * 512, 512), 512)]
        result = nn(normed_t[...], block).astype(BF16)
        for n in range(4):
            pt[i, two * 2 + n // 2, n % 2] = result[:, n * 128:(n + 1) * 128]

    def terms(d):
        i = (x + d) % 4
        for two in range(2):
            term(i, two)
        pair_copy(i).start()

    terms(1)
    terms(2)
    arrived(wc_second)
    wc_last = go([remote(wc.at[:, :, c], wc.at[:, :, c], wcs_s.at[0], wcs_r.at[0], sibling)])

    arrived(wr_first)
    wr_second = go(
        [
            remote(
                wr.at[:, y, c, :, pl.ds(0, 16)], wr.at[:, y, c, :, pl.ds(0, 16)],
                wr2_s.at[d - 1], wr2_r.at[d - 1], y_dev(d),
            )
            for d in (1, 3, 2)
        ]
        + [
            remote(
                wr.at[:, :, c, x, pl.ds(16, 16)], wr.at[:, :, c, x, pl.ds(16, 16)],
                wr2_s.at[2 + d], wr2_r.at[2 + d], x_dev(d),
            )
            for d in (1, 3, 2)
        ]
    )

    terms(3)

    arrived(wc_last)

    @pl.loop(0, 2)
    def _(two):
        both = pl.ds(pl.multiple_of(two * 512, 512), 512)
        g_all = nn(og[both, :], wc[...].reshape(WIDTH, COLS))
        for part in range(2):
            t = two * 2 + part
            for h in range(HEADS):
                g = g_all[part * CHUNK:(part + 1) * CHUNK, head_cols(h)]
                n = nf[rows_of(t), head_cols(h)]
                inner = jnp.mean(n * g, axis=-1, keepdims=True)
                grad = (inv[rows_of(t), head_cols(h)] * (g - n * inner)).astype(BF16)
                ga[rows_of(t), head_cols(h)] = grad
                qdas[t, h] = tn(q[rows_of(t), head_cols(h)], grad)

    publish(1, qdas)
    step = scan_first(1)
    forward(0)
    forward(1)

    def inner_gradients(t):
        for h in range(HEADS):
            where = (rows_of(t), head_cols(h))
            qh, kh, vh, gh = q[where], k[where], v[where], ga[where]
            dmask = lower(nt(gh, vh))
            gq[where] = (nn(dmask, kh) + nt(gh, states[t, h])).astype(BF16)
            dmask_t = upper(nt(vh, gh))
            att[where] = nn(dmask_t, qh)
            nf[where] = nn(masked_t[t, h], gh)

    def x_final(d):
        return remote(
            qb.at[(x + d) % 4], r2b.at[d - 1], rs2_s.at[1, d - 1], rs2_r.at[1, d - 1], x_dev(d)
        )

    def y_final(d):
        return remote(
            qa.at[(y + d) % 4], r2a.at[d - 1], rs2_s.at[0, d - 1], rs2_r.at[0, d - 1], y_dev(d)
        )

    terms(0)
    arrived(step)
    step = scan_second(1)
    pl.loop(0, 3)(inner_gradients)
    arrived(step)
    step = scan_third(1)

    def x_part(d):
        return remote(
            pt.at[(x + d) % 4, :, c, pl.ds(0, 256)], ra.at[d - 1],
            rs1_s.at[0, d - 1], rs1_r.at[0, d - 1], x_dev(d),
        )

    for d in range(1, 5):
        i = (x + d) % 4
        pair_copy(i).wait_recv()

        @pl.loop(0, 4)
        def _(j):
            pt[i, j, c] = (pt[i, j, c].astype(F32) + r0[i, j].astype(F32)).astype(BF16)

        if d < 4:
            x_part(d).start()

    def y_part(d):
        return remote(
            pt.at[:, (y + d) % 4, c, pl.ds(256, 256)], rb.at[d - 1],
            rs1_s.at[1, d - 1], rs1_r.at[1, d - 1], y_dev(d),
        )

    for d in (1, 3, 2):
        y_part(d).start()

    pl.loop(3, CHUNKS)(inner_gradients)
    forward(2)
    forward(3)
    arrived(wr_second)
    wr_last = go([remote(wr.at[:, :, c], wr.at[:, :, c], wrs_s.at[0], wrs_r.at[0], sibling)])
    arrived(step)
    step = scan_fourth(1)
    arrived(step)

    for h in range(HEADS):
        state = incoming(1, h)
        for t in range(CHUNKS - 1, -1, -1):
            futures[t, h] = state.astype(BF16)
            state = state + qdas[t, h]

    @pl.loop(0, CHUNKS)
    def _(t):
        for h in range(HEADS):
            where = (rows_of(t), head_cols(h))
            gk[where] = (att[where] + nt(v[where], futures[t, h])).astype(BF16)
            gv[where] = (nf[where] + nn(k[where], futures[t, h])).astype(BF16)

    arrived(wr_last)

    @pl.loop(0, 2)
    def _(two):
        both = pl.ds(pl.multiple_of(two * 512, 512), 512)
        result = nt(nb[0, both], wc[z].reshape(TOK, COLS))
        for d in (1, 3):
            result = result + nt(nb[d, both], wr[d - 1].reshape(TOK, COLS))
        acc[both, :] = result

    for d in range(1, 4):
        x_part(d).wait_recv()
    for j in range(4):
        summed = pt[x, j, c, :256, :].astype(F32)
        for d in range(3):
            summed = summed + ra[d, j].astype(F32)
        qa[j] = summed.astype(BF16)

    finals = go([y_final(d) for d in (1, 3, 2)])
    for d in range(1, 4):
        y_part(d).wait_recv()
    for j in range(4):
        summed = pt[j, y, c, 256:, :].astype(F32)
        for d in range(3):
            summed = summed + rb[d, j].astype(F32)
        qb[j] = summed.astype(BF16)
    finals += go([x_final(d) for d in (1, 3, 2)])
    @pl.loop(0, CHUNKS)
    def _(t):
        for way in (0, 1):
            z_forward(t, way).wait_recv()
        result = acc[rows_of(t), :] + nt(nb[2, rows_of(t)], wr[1].reshape(TOK, COLS))
        mixed[rows_of(t), :] = result.astype(BF16)

    arrived(finals)
    for half, own, others in ((0, qa[y], r2a), (1, qb[x], r2b)):
        summed = own.astype(F32)
        for d in range(3):
            summed = summed + others[d].astype(F32)
        gw[:, half * 256:(half + 1) * 256] = summed.T

    for copy in pending:
        copy.wait_send()

    @pl.loop(0, CHUNKS)
    def _(t):
        for way in (0, 1):
            z_send(t, way).wait_send()
            z_forward(t, way).wait_send()

    for i in range(4):
        pair_copy(i).wait_send()

    for d in range(1, 4):
        x_part(d).wait_send()
        y_part(d).wait_send()


def deliver(*refs):
    copies = [
        pltpu.make_async_copy(source, target, refs[10].at[i])
        for i, (source, target) in enumerate(zip(refs[:5], refs[5:10]))
    ]
    for copy in copies:
        copy.start()
    for copy in copies:
        copy.wait()


def per_device(queries, keys, values, out_weight, out_grad):
    dma = pltpu.SemaphoreType.DMA
    vm = pltpu.VMEM
    scratch = [
        vm((TOK, COLS), BF16),
        vm((TOK, COLS), BF16),
        vm((TOK, COLS), BF16),
        vm((TOK, WIDTH), BF16),
        vm((4, 4, 2, 128, COLS), BF16),
        vm((4, 32, COLS), BF16),
        vm((3, 4, 2, 4, 32, COLS), BF16),
        vm((4, TOK, COLS), BF16),
        vm((COLS, TOK), BF16),
        vm((CHUNKS, HEADS, CHUNK, CHUNK), BF16),
        vm((TOK, COLS), F32),
        vm((TOK, COLS), F32),
        vm((TOK, COLS), F32),
        vm((CHUNKS, HEADS, 128, 128), F32),
        vm((CHUNKS, HEADS, 128, 128), BF16),
        vm((TOK, COLS), BF16),
        vm((CHUNKS, HEADS, 128, 128), F32),
        vm((CHUNKS, HEADS, 128, 128), BF16),
        vm((2, 2, 16, 16, 128), BF16),
        vm((2, 16, 16, 128), BF16),
        vm((2, 16, 16, 128), BF16),
        vm((2, 16, 16, 128), BF16),
        vm((2, 16, 16, 128), BF16),
        vm((2, 16, 16, 128), BF16),
        vm((2, 16, 16, 128), BF16),
        vm((2, 2, 16, 16, 128), BF16),
        vm((4, 4, 2, COLS, 128), BF16),
        vm((4, 4, COLS, 128), BF16),
        vm((3, 4, 256, 128), BF16),
        vm((3, 4, 256, 128), BF16),
        vm((4, 256, 128), BF16),
        vm((4, 256, 128), BF16),
        vm((3, 256, 128), BF16),
        vm((3, 256, 128), BF16),
        vm((TOK, 1024), F32),
        dma((5,)),
    ]
    pairs = [
        (6,), (6,), (1,),
        (3,), (3,), (6,), (6,), (1,),
        (2, 1), (2,), (2,), (2, 1),
        (2, CHUNKS), (2, CHUNKS),
        (4,), (2, 3), (2, 3),
    ]
    for shape in pairs:
        scratch += [dma(shape), dma(shape)]
    anywhere = pl.BlockSpec(memory_space=pl.ANY)
    shapes = (
        jax.ShapeDtypeStruct((TOK, 1024), BF16),
        jax.ShapeDtypeStruct((TOK, COLS), BF16),
        jax.ShapeDtypeStruct((TOK, COLS), BF16),
        jax.ShapeDtypeStruct((TOK, COLS), BF16),
        jax.ShapeDtypeStruct((128, COLS), F32),
    )
    results = pl.pallas_call(
        kernel,
        out_shape=tuple(vm(shape.shape, shape.dtype) for shape in shapes),
        in_specs=[anywhere] * 5,
        out_specs=(pl.BlockSpec(memory_space=vm),) * 5,
        scratch_shapes=scratch,
        compiler_params=pltpu.CompilerParams(
            collective_id=0, has_side_effects=True, vmem_limit_bytes=52 << 20
        ),
    )(queries, keys, values, out_weight, out_grad)
    return pl.pallas_call(
        deliver,
        out_shape=shapes,
        in_specs=[pl.BlockSpec(memory_space=vm)] * 5,
        out_specs=(anywhere,) * 5,
        scratch_shapes=[dma((5,))],
        compiler_params=pltpu.CompilerParams(vmem_limit_bytes=4 << 20),
    )(*results)


def solution(mesh):
    in_specs = (
        P("seq", "head"),
        P("seq", "head"),
        P("seq", "head"),
        P("seq", "head"),
        P("seq", None),
    )
    out_specs = (
        P("seq", "head"),
        P("seq", "head"),
        P("seq", "head"),
        P("seq", "head"),
        P("seq", "head"),
    )
    return jax.shard_map(
        per_device, mesh=mesh, in_specs=in_specs, out_specs=out_specs, check_vma=False
    )
```

```python
import jax
import jax.numpy as jnp
from jax import lax
from jax.experimental import pallas as pl
from jax.experimental.pallas import tpu as pltpu
from jax.sharding import PartitionSpec as P

HEAD_DIM = 128
HEADS = 4
CHUNK = 256
CHUNKS = 4
TOK = 1024
COLS = 512
WIDTH = 4096
EPSILON = 1e-06
MESH = pl.DeviceIdType.MESH
F32 = jnp.float32
BF16 = jnp.bfloat16


def nn(a, b):
    return lax.dot_general(a, b, (((1,), (0,)), ((), ())), preferred_element_type=F32)


def nt(a, b):
    return lax.dot_general(a, b, (((1,), (1,)), ((), ())), preferred_element_type=F32)


def tn(a, b):
    return lax.dot_general(a, b, (((0,), (0,)), ((), ())), preferred_element_type=F32)


def kernel(
    q_hbm, k_hbm, v_hbm, w_hbm, og_hbm,
    mixed, gq, gk, gv, gw,
    q, k, v, og, wc, quarter, wr, nb, normed_t, masked_t, att, nf, inv,
    kvs, states, ga, qdas, futures, own_state, peer, chip_state, slices, offset, before, back, final,
    pt, r0, ra, rb, qa, qb, r2a, r2b, acc,
    load_sem,
    wc1_s, wc1_r, wc2_s, wc2_r, wcs_s, wcs_r,
    wq_s, wq_r, wz_s, wz_r, wr1_s, wr1_r, wr2_s, wr2_r, wrs_s, wrs_r,
    sc1_s, sc1_r, sc2_s, sc2_r, sc3_s, sc3_r, sc4_s, sc4_r,
    zs_s, zs_r, zf_s, zf_r,
    rs0_s, rs0_r, rs1_s, rs1_r, rs2_s, rs2_r,
):
    seq = lax.axis_index("seq")
    z = lax.axis_index("head")
    x, y, c = seq // 8, (seq // 2) % 4, seq % 2
    chip = x * 4 + y

    def at(x_, y_, c_, z_):
        return (x_ * 8 + y_ * 2 + c_, z_)

    def x_dev(d):
        return at((x + d) % 4, y, c, z)

    def y_dev(d):
        return at(x, (y + d) % 4, c, z)

    def z_dev(d):
        return (seq, (z + d) % 4)

    def plane_dev(m):
        other = (chip + m) % 16
        return at(other // 4, other % 4, c, z)

    sibling = at(x, y, 1 - c, z)

    def remote(src, dst, send, recv, device):
        return pltpu.make_async_remote_copy(
            src_ref=src, dst_ref=dst, send_sem=send, recv_sem=recv,
            device_id=device, device_id_type=MESH,
        )

    pending = []

    def go(copies):
        for copy in copies:
            copy.start()
            pending.append(copy)
        return copies

    def arrived(copies):
        for copy in copies:
            copy.wait_recv()

    loads = [
        pltpu.make_async_copy(w_hbm, wc.at[x, y, c], load_sem.at[0]),
        pltpu.make_async_copy(k_hbm, k, load_sem.at[1]),
        pltpu.make_async_copy(v_hbm, v, load_sem.at[2]),
        pltpu.make_async_copy(q_hbm, q, load_sem.at[3]),
        pltpu.make_async_copy(og_hbm, og, load_sem.at[4]),
    ]
    for load in loads[:4]:
        load.start()

    barrier = pltpu.get_barrier_semaphore()
    partners = [plane_dev(m) for m in range(1, 16)] + [sibling, z_dev(1), z_dev(2), z_dev(3)]
    for partner in partners:
        pl.semaphore_signal(barrier, inc=1, device_id=partner, device_id_type=MESH)

    def rows_of(t):
        return pl.ds(pl.multiple_of(t * CHUNK, CHUNK), CHUNK)

    def head_cols(h):
        return slice(h * HEAD_DIM, (h + 1) * HEAD_DIM)

    loads[1].wait()
    loads[2].wait()
    loads[3].wait()
    loads[4].start()

    @pl.loop(0, CHUNKS)
    def _(t):
        for h in range(HEADS):
            kvs[t, h] = tn(k[rows_of(t), head_cols(h)], v[rows_of(t), head_cols(h)])

    def publish(n, source):
        for h in range(HEADS):
            state = source[0, h] + source[1, h] + source[2, h] + source[3, h]
            own_state[n, h // 2, (h % 2) * 8:(h % 2) * 8 + 8] = (
                state.astype(BF16).reshape(8, 16, HEAD_DIM)
            )

    def scan_first(n):
        return go(
            [remote(own_state.at[n, 1 - c], peer.at[n], sc1_s.at[n, 0], sc1_r.at[n, 0], sibling)]
        )

    def scan_second(n):
        chip_state[n] = (own_state[n, c].astype(F32) + peer[n].astype(F32)).astype(BF16)
        for m in range(1, 16):
            remote(
                chip_state.at[n, (chip + m) % 16], slices.at[n, chip],
                sc2_s.at[n], sc2_r.at[n], plane_dev(m),
            ).start()
        whole = remote(
            chip_state.at[n, pl.ds(0, 15)], slices.at[n, pl.ds(0, 15)],
            sc2_s.at[n], sc2_r.at[n], plane_dev(1),
        )
        pending.append(whole)
        slices[n, chip] = chip_state[n, chip]
        return [whole]

    def scan_third(n):
        base = jnp.zeros((16, HEAD_DIM), F32)
        for i in range(16) if n == 0 else range(15, -1, -1):
            offset[n, i] = base.astype(BF16)
            base = base + slices[n, i].astype(F32)
        for m in range(1, 16):
            remote(
                offset.at[n, (chip + m) % 16], before.at[n, chip],
                sc3_s.at[n], sc3_r.at[n], plane_dev(m),
            ).start()
        whole = remote(
            offset.at[n, pl.ds(0, 15)], before.at[n, pl.ds(0, 15)],
            sc3_s.at[n], sc3_r.at[n], plane_dev(1),
        )
        pending.append(whole)
        before[n, chip] = offset[n, chip]
        return [whole]

    def scan_fourth(n):
        base = before[n].astype(F32)
        self_second, other_second = (c == 1, c == 0) if n == 0 else (c == 0, c == 1)
        back[n] = (base + jnp.where(other_second, own_state[n, c].astype(F32), 0.0)).astype(BF16)
        copies = go(
            [remote(back.at[n], final.at[n, c], sc4_s.at[n, 0], sc4_r.at[n, 0], sibling)]
        )
        final[n, c] = (base + jnp.where(self_second, peer[n].astype(F32), 0.0)).astype(BF16)
        return copies

    def incoming(n, h):
        half = final[n, h // 2, (h % 2) * 8:(h % 2) * 8 + 8].astype(F32)
        return half.reshape(HEAD_DIM, HEAD_DIM)

    publish(0, kvs)
    pl.semaphore_wait(barrier, len(partners))
    step = scan_first(0)

    loads[0].wait()
    wc_first = go(
        [
            remote(
                wc.at[x, y, c, pl.ds(0, 64)], wc.at[x, y, c, pl.ds(0, 64)],
                wc1_s.at[d - 1], wc1_r.at[d - 1], x_dev(d),
            )
            for d in (1, 3, 2)
        ]
        + [
            remote(
                wc.at[x, y, c, pl.ds(64, 64)], wc.at[x, y, c, pl.ds(64, 64)],
                wc1_s.at[2 + d], wc1_r.at[2 + d], y_dev(d),
            )
            for d in (1, 3, 2)
        ]
    )

    def quarter_rows(part):
        return pl.ds(pl.multiple_of(part * 32, 32), 32)

    quarters = go(
        [
            remote(
                wc.at[x, y, c, quarter_rows((x + d) % 4)], quarter.at[x],
                wq_s.at[d - 1], wq_r.at[d - 1], x_dev(d),
            )
            for d in (1, 3, 2)
        ]
    )
    quarter[x] = wc[x, y, c, quarter_rows(x), :]

    row = lax.broadcasted_iota(jnp.int32, (CHUNK, CHUNK), 0)
    col = lax.broadcasted_iota(jnp.int32, (CHUNK, CHUNK), 1)

    def lower(scores):
        return jnp.where(row >= col, scores, 0.0).astype(BF16)

    def upper(scores):
        return jnp.where(row <= col, scores, 0.0).astype(BF16)

    def intra(t):
        for h in range(HEADS):
            qh, kh = q[rows_of(t), head_cols(h)], k[rows_of(t), head_cols(h)]
            att[rows_of(t), head_cols(h)] = nn(lower(nt(qh, kh)), v[rows_of(t), head_cols(h)])

    pl.loop(0, 1)(intra)
    arrived(step)
    step = scan_second(0)
    pl.loop(1, CHUNKS)(intra)
    arrived(step)
    step = scan_third(0)
    arrived(wc_first)
    arrived(quarters)

    wc_second = go(
        [
            remote(
                wc.at[:, y, c, pl.ds(0, 64)], wc.at[:, y, c, pl.ds(0, 64)],
                wc2_s.at[d - 1], wc2_r.at[d - 1], y_dev(d),
            )
            for d in (1, 3, 2)
        ]
        + [
            remote(
                wc.at[x, :, c, pl.ds(64, 64)], wc.at[x, :, c, pl.ds(64, 64)],
                wc2_s.at[2 + d], wc2_r.at[2 + d], x_dev(d),
            )
            for d in (1, 3, 2)
        ]
    )

    to_layer = go(
        [
            remote(
                quarter.at[(z + d) % 4], wr.at[3 - d, y, c, x],
                wz_s.at[d - 1], wz_r.at[d - 1], z_dev(d),
            )
            for d in (1, 3, 2)
        ]
    )

    @pl.loop(0, CHUNKS)
    def _(t):
        for h in range(HEADS):
            masked_t[t, h] = upper(nt(k[rows_of(t), head_cols(h)], q[rows_of(t), head_cols(h)]))

    arrived(step)
    step = scan_fourth(0)
    arrived(step)

    for h in range(HEADS):
        state = incoming(0, h)
        for t in range(CHUNKS):
            states[t, h] = state.astype(BF16)
            state = state + kvs[t, h]

    def z_send(t, way):
        return remote(
            nb.at[0, rows_of(t)], nb.at[3 if way == 0 else 1, rows_of(t)],
            zs_s.at[way, t], zs_r.at[way, t], z_dev(1 if way == 0 else 3),
        )

    def z_forward(t, way):
        part = pl.ds(pl.multiple_of(t * CHUNK + way * 128, 128), 128)
        return remote(
            nb.at[3 if way == 0 else 1, part], nb.at[2, part],
            zf_s.at[way, t], zf_r.at[way, t], z_dev(1 if way == 0 else 3),
        )

    def forward(t):
        for way in (0, 1):
            z_send(t, way).wait_recv()
            z_forward(t, way).start()

    @pl.loop(0, CHUNKS)
    def _(t):
        for h in range(HEADS):
            a = att[rows_of(t), head_cols(h)] + nn(q[rows_of(t), head_cols(h)], states[t, h])
            scale = lax.rsqrt(jnp.mean(a * a, axis=-1, keepdims=True) + EPSILON)
            n = a * scale
            nf[rows_of(t), head_cols(h)] = n
            inv[rows_of(t), head_cols(h)] = jnp.broadcast_to(scale, n.shape)
            nb[0, rows_of(t), head_cols(h)] = n.astype(BF16)
            normed_t[head_cols(h), rows_of(t)] = n.T.astype(BF16)
        for way in (0, 1):
            z_send(t, way).start()

    arrived(to_layer)
    wr_first = go(
        [
            remote(
                wr.at[:, y, c, x, pl.ds(0, 16)], wr.at[:, y, c, x, pl.ds(0, 16)],
                wr1_s.at[d - 1], wr1_r.at[d - 1], x_dev(d),
            )
            for d in (1, 3, 2)
        ]
        + [
            remote(
                wr.at[:, y, c, x, pl.ds(16, 16)], wr.at[:, y, c, x, pl.ds(16, 16)],
                wr1_s.at[2 + d], wr1_r.at[2 + d], y_dev(d),
            )
            for d in (1, 3, 2)
        ]
    )

    def pair_copy(i):
        return remote(
            pt.at[i, :, 1 - c], r0.at[i], rs0_s.at[i], rs0_r.at[i], sibling
        )

    loads[4].wait()

    def term(i, two):
        block = og[:, pl.ds(pl.multiple_of((i * 2 + two) * 512, 512), 512)]
        result = nn(normed_t[...], block).astype(BF16)
        for n in range(4):
            pt[i, two * 2 + n // 2, n % 2] = result[:, n * 128:(n + 1) * 128]

    def terms(d):
        i = (x + d) % 4
        for two in range(2):
            term(i, two)
        pair_copy(i).start()

    terms(1)
    terms(2)
    terms(3)
    arrived(wc_second)
    wc_last = go([remote(wc.at[:, :, c], wc.at[:, :, c], wcs_s.at[0], wcs_r.at[0], sibling)])

    arrived(wr_first)
    wr_second = go(
        [
            remote(
                wr.at[:, y, c, :, pl.ds(0, 16)], wr.at[:, y, c, :, pl.ds(0, 16)],
                wr2_s.at[d - 1], wr2_r.at[d - 1], y_dev(d),
            )
            for d in (1, 3, 2)
        ]
        + [
            remote(
                wr.at[:, :, c, x, pl.ds(16, 16)], wr.at[:, :, c, x, pl.ds(16, 16)],
                wr2_s.at[2 + d], wr2_r.at[2 + d], x_dev(d),
            )
            for d in (1, 3, 2)
        ]
    )

    terms(0)

    arrived(wc_last)

    @pl.loop(0, 2)
    def _(two):
        both = pl.ds(pl.multiple_of(two * 512, 512), 512)
        g_all = nn(og[both, :], wc[...].reshape(WIDTH, COLS))
        for part in range(2):
            t = two * 2 + part
            for h in range(HEADS):
                g = g_all[part * CHUNK:(part + 1) * CHUNK, head_cols(h)]
                n = nf[rows_of(t), head_cols(h)]
                inner = jnp.mean(n * g, axis=-1, keepdims=True)
                grad = (inv[rows_of(t), head_cols(h)] * (g - n * inner)).astype(BF16)
                ga[rows_of(t), head_cols(h)] = grad
                qdas[t, h] = tn(q[rows_of(t), head_cols(h)], grad)

    publish(1, qdas)
    step = scan_first(1)
    forward(0)
    forward(1)

    def inner_gradients(t):
        for h in range(HEADS):
            where = (rows_of(t), head_cols(h))
            qh, kh, vh, gh = q[where], k[where], v[where], ga[where]
            dmask = lower(nt(gh, vh))
            gq[where] = (nn(dmask, kh) + nt(gh, states[t, h])).astype(BF16)
            dmask_t = upper(nt(vh, gh))
            att[where] = nn(dmask_t, qh)
            nf[where] = nn(masked_t[t, h], gh)

    def x_final(d):
        return remote(
            qb.at[(x + d) % 4], r2b.at[d - 1], rs2_s.at[1, d - 1], rs2_r.at[1, d - 1], x_dev(d)
        )

    def y_final(d):
        return remote(
            qa.at[(y + d) % 4], r2a.at[d - 1], rs2_s.at[0, d - 1], rs2_r.at[0, d - 1], y_dev(d)
        )

    arrived(step)
    step = scan_second(1)
    pl.loop(0, 3)(inner_gradients)
    arrived(step)
    step = scan_third(1)

    def x_part(d):
        return remote(
            pt.at[(x + d) % 4, :, c, pl.ds(0, 256)], ra.at[d - 1],
            rs1_s.at[0, d - 1], rs1_r.at[0, d - 1], x_dev(d),
        )

    for d in range(1, 5):
        i = (x + d) % 4
        pair_copy(i).wait_recv()

        @pl.loop(0, 4)
        def _(j):
            pt[i, j, c] = (pt[i, j, c].astype(F32) + r0[i, j].astype(F32)).astype(BF16)

        if d < 4:
            x_part(d).start()

    def y_part(d):
        return remote(
            pt.at[:, (y + d) % 4, c, pl.ds(256, 256)], rb.at[d - 1],
            rs1_s.at[1, d - 1], rs1_r.at[1, d - 1], y_dev(d),
        )

    for d in (1, 3, 2):
        y_part(d).start()

    pl.loop(3, CHUNKS)(inner_gradients)
    forward(2)
    forward(3)
    arrived(wr_second)
    wr_last = go([remote(wr.at[:, :, c], wr.at[:, :, c], wrs_s.at[0], wrs_r.at[0], sibling)])
    arrived(step)
    step = scan_fourth(1)
    arrived(step)

    for h in range(HEADS):
        state = incoming(1, h)
        for t in range(CHUNKS - 1, -1, -1):
            futures[t, h] = state.astype(BF16)
            state = state + qdas[t, h]

    @pl.loop(0, CHUNKS)
    def _(t):
        for h in range(HEADS):
            where = (rows_of(t), head_cols(h))
            gk[where] = (att[where] + nt(v[where], futures[t, h])).astype(BF16)
            gv[where] = (nf[where] + nn(k[where], futures[t, h])).astype(BF16)

    arrived(wr_last)

    @pl.loop(0, 2)
    def _(two):
        both = pl.ds(pl.multiple_of(two * 512, 512), 512)
        result = nt(nb[0, both], wc[z].reshape(TOK, COLS))
        for d in (1, 3):
            result = result + nt(nb[d, both], wr[d - 1].reshape(TOK, COLS))
        acc[both, :] = result

    for d in range(1, 4):
        x_part(d).wait_recv()
    for j in range(4):
        summed = pt[x, j, c, :256, :].astype(F32)
        for d in range(3):
            summed = summed + ra[d, j].astype(F32)
        qa[j] = summed.astype(BF16)

    finals = go([y_final(d) for d in (1, 3, 2)])
    for d in range(1, 4):
        y_part(d).wait_recv()
    for j in range(4):
        summed = pt[j, y, c, 256:, :].astype(F32)
        for d in range(3):
            summed = summed + rb[d, j].astype(F32)
        qb[j] = summed.astype(BF16)
    finals += go([x_final(d) for d in (1, 3, 2)])
    @pl.loop(0, CHUNKS)
    def _(t):
        for way in (0, 1):
            z_forward(t, way).wait_recv()
        result = acc[rows_of(t), :] + nt(nb[2, rows_of(t)], wr[1].reshape(TOK, COLS))
        mixed[rows_of(t), :] = result.astype(BF16)

    arrived(finals)
    for half, own, others in ((0, qa[y], r2a), (1, qb[x], r2b)):
        summed = own.astype(F32)
        for d in range(3):
            summed = summed + others[d].astype(F32)
        gw[:, half * 256:(half + 1) * 256] = summed.T

    for copy in pending:
        copy.wait_send()

    @pl.loop(0, CHUNKS)
    def _(t):
        for way in (0, 1):
            z_send(t, way).wait_send()
            z_forward(t, way).wait_send()

    for i in range(4):
        pair_copy(i).wait_send()

    for d in range(1, 4):
        x_part(d).wait_send()
        y_part(d).wait_send()


def deliver(*refs):
    copies = [
        pltpu.make_async_copy(source, target, refs[10].at[i])
        for i, (source, target) in enumerate(zip(refs[:5], refs[5:10]))
    ]
    for copy in copies:
        copy.start()
    for copy in copies:
        copy.wait()


def per_device(queries, keys, values, out_weight, out_grad):
    dma = pltpu.SemaphoreType.DMA
    vm = pltpu.VMEM
    scratch = [
        vm((TOK, COLS), BF16),
        vm((TOK, COLS), BF16),
        vm((TOK, COLS), BF16),
        vm((TOK, WIDTH), BF16),
        vm((4, 4, 2, 128, COLS), BF16),
        vm((4, 32, COLS), BF16),
        vm((3, 4, 2, 4, 32, COLS), BF16),
        vm((4, TOK, COLS), BF16),
        vm((COLS, TOK), BF16),
        vm((CHUNKS, HEADS, CHUNK, CHUNK), BF16),
        vm((TOK, COLS), F32),
        vm((TOK, COLS), F32),
        vm((TOK, COLS), F32),
        vm((CHUNKS, HEADS, 128, 128), F32),
        vm((CHUNKS, HEADS, 128, 128), BF16),
        vm((TOK, COLS), BF16),
        vm((CHUNKS, HEADS, 128, 128), F32),
        vm((CHUNKS, HEADS, 128, 128), BF16),
        vm((2, 2, 16, 16, 128), BF16),
        vm((2, 16, 16, 128), BF16),
        vm((2, 16, 16, 128), BF16),
        vm((2, 16, 16, 128), BF16),
        vm((2, 16, 16, 128), BF16),
        vm((2, 16, 16, 128), BF16),
        vm((2, 16, 16, 128), BF16),
        vm((2, 2, 16, 16, 128), BF16),
        vm((4, 4, 2, COLS, 128), BF16),
        vm((4, 4, COLS, 128), BF16),
        vm((3, 4, 256, 128), BF16),
        vm((3, 4, 256, 128), BF16),
        vm((4, 256, 128), BF16),
        vm((4, 256, 128), BF16),
        vm((3, 256, 128), BF16),
        vm((3, 256, 128), BF16),
        vm((TOK, 1024), F32),
        dma((5,)),
    ]
    pairs = [
        (6,), (6,), (1,),
        (3,), (3,), (6,), (6,), (1,),
        (2, 1), (2,), (2,), (2, 1),
        (2, CHUNKS), (2, CHUNKS),
        (4,), (2, 3), (2, 3),
    ]
    for shape in pairs:
        scratch += [dma(shape), dma(shape)]
    anywhere = pl.BlockSpec(memory_space=pl.ANY)
    shapes = (
        jax.ShapeDtypeStruct((TOK, 1024), BF16),
        jax.ShapeDtypeStruct((TOK, COLS), BF16),
        jax.ShapeDtypeStruct((TOK, COLS), BF16),
        jax.ShapeDtypeStruct((TOK, COLS), BF16),
        jax.ShapeDtypeStruct((128, COLS), F32),
    )
    results = pl.pallas_call(
        kernel,
        out_shape=tuple(vm(shape.shape, shape.dtype) for shape in shapes),
        in_specs=[anywhere] * 5,
        out_specs=(pl.BlockSpec(memory_space=vm),) * 5,
        scratch_shapes=scratch,
        compiler_params=pltpu.CompilerParams(
            collective_id=0, has_side_effects=True, vmem_limit_bytes=52 << 20
        ),
    )(queries, keys, values, out_weight, out_grad)
    return pl.pallas_call(
        deliver,
        out_shape=shapes,
        in_specs=[pl.BlockSpec(memory_space=vm)] * 5,
        out_specs=(anywhere,) * 5,
        scratch_shapes=[dma((5,))],
        compiler_params=pltpu.CompilerParams(vmem_limit_bytes=4 << 20),
    )(*results)


def solution(mesh):
    in_specs = (
        P("seq", "head"),
        P("seq", "head"),
        P("seq", "head"),
        P("seq", "head"),
        P("seq", None),
    )
    out_specs = (
        P("seq", "head"),
        P("seq", "head"),
        P("seq", "head"),
        P("seq", "head"),
        P("seq", "head"),
    )
    return jax.shard_map(
        per_device, mesh=mesh, in_specs=in_specs, out_specs=out_specs, check_vma=False
    )
```
